32 devices in a mesh: groups: 2 (over x), dp: 16 (over z, y, core).
Axes of the slice: x: 2, y: 2, z: 4, core: 2. Of those that a mesh axis runs over, the one named last changes fastest.
Arguments:
- tokens: bfloat16 [8192, 8192], P(('groups', 'dp')), parts along dimension 0, may hold values from -6 to 6
- output_gradient: bfloat16 [8192, 1024], P(('groups', 'dp')), parts along dimension 0, may hold values from -6 to 6
- adapter_hidden_state: bfloat16 [8192, 64], P(('groups', 'dp')), parts along dimension 0, may hold values from -6 to 6
- frozen_value_weight: bfloat16 [8192, 1024], P('dp'), may hold values from -0.1875 to 0.1875
- adapter_down_maps: bfloat16 [16384, 256], P(('groups', 'dp')), parts along dimension 0, may hold values from -0.75 to 0.75
- adapter_up_maps: bfloat16 [512, 1024], P('groups'), parts along dimension 0, may hold values from -0.1875 to 0.1875
- members: int32 [64], P('groups'), parts along dimension 0, may hold values from 0 to 3, never falling along the last dimension, each value on 1 to 16 neighbouring positions
Outputs:
- layer_input_gradient: bfloat16 [8192, 8192], P(('groups', 'dp')), parts along dimension 0
- down_grad: float32 [16384, 256], P(('groups', 'dp')), parts along dimension 0
- up_map_gradient: float32 [512, 1024], P('groups'), parts along dimension 0
The draws below stay inside these ranges and needn't reach their ends.
There are 2 independent parts, one for each index of `groups`. The reference program is written for one: setup_inputs(seed, part) draws one part's arguments, and reference() takes and returns one part's arrays. A program takes and returns all parts, laid end to end along the dimension named above; an argument that names none is the same for every part. Nothing has to cross between parts.
Inputs may be any that keep to these rules, and one draw needn't show every extreme that they name: members never falls from one block to the next, and every member owns at least one block.
All inputs are finite; a program needn't handle non-finite values.
Results may differ from the reference program's by a relative error of at most 0.008.
Values may be sent and summed in bfloat16 or wider, within the bound.
No kernel may reach another device: no remote copies, remote signals or barrier semaphores. Data moves between devices by JAX's collectives and lax.ppermute only.
A program may use at most 128 MiB of HBM per device.

```python
import math
import jax
import jax.numpy as jnp
import numpy as np
from jax import lax

MODEL_WIDTH = 8192
VALUE_WIDTH = 1024
ADAPTER_RANK = 64
MEMBER_COUNT = 4
BLOCK = 128
TOKENS = 4096
BLOCKS = 32


def block_levels(rng, extent, split, least, top_value):
    level = 1.0
    for dim, blocks in split:
        draws = jax.random.uniform(jax.random.fold_in(jax.random.fold_in(rng, 6), dim), (blocks,), jnp.float32, least / len(split), top_value / len(split))
        level = level * jnp.repeat(jnp.exp(draws), extent[dim] // blocks).reshape((-1,) + (1,) * (len(extent) - 1 - dim))
    return level


def split_up(count, total, limit, slope):
    loads = [(1 << 20) // math.isqrt(rank ** slope) + 1 for rank in range(2, count + 1)]
    spare, counts = total - limit - (count - 1), [1] * (count - 1)
    while spare > 0:
        movable = [i for i in range(count - 1) if counts[i] < limit]
        pool, left = sum([loads[i] for i in movable]), spare
        for i in movable:
            more = min(limit - counts[i], max(1, left * loads[i] // pool), spare)
            counts[i] = counts[i] + more
            spare = spare - more
    return np.array([limit] + counts)


def uneven(stream_key, number_of, total, bound, slope):
    if number_of == 2:
        one = jax.random.randint(stream_key, (), max(1, total - bound), min(bound, total - 1) + 1)
        return jnp.stack([one, total - one])
    tallies = jnp.asarray(split_up(number_of, total, bound, slope), jnp.int32)
    couples = (number_of - 1) // 2
    source_of, taker = tallies[1:1 + 2 * couples:2], tallies[2:2 + 2 * couples:2]
    margin = jnp.minimum(source_of - 1, bound - taker)
    moved = jax.random.randint(jax.random.fold_in(stream_key, 1), (couples,), 0, 1 << 20) % (margin + 1)
    tallies = tallies.at[1:1 + 2 * couples:2].set(source_of - moved).at[2:2 + 2 * couples:2].set(taker + moved)
    return tallies[jax.random.permutation(jax.random.fold_in(stream_key, 2), number_of)]


def scatter_about(rng, dims, spread, bound, cuts=(), held_as=jnp.bfloat16):
    result = spread * jax.random.normal(rng, dims, jnp.float32)
    if cuts:
        result = result * block_levels(rng, dims, cuts, -0.22, 0.18)
    return jnp.clip(result, -bound, bound).astype(held_as)


def setup_inputs(seed: int = 0, part: int = 0) -> dict:
    key_list = jax.random.split(jax.random.key(seed), 8)
    part_splits = jax.random.split(jax.random.fold_in(key_list[7], part), 8)
    return {
        "tokens": scatter_about(part_splits[0], (TOKENS, MODEL_WIDTH), 1.0, 6.0, ((0, 16),)),
        "output_gradient": scatter_about(part_splits[1], (TOKENS, VALUE_WIDTH), 1.0, 6.0, ((0, 16),)),
        "adapter_hidden_state": scatter_about(part_splits[2], (TOKENS, ADAPTER_RANK), 1.0, 6.0, ((0, 16),)),
        "frozen_value_weight": scatter_about(key_list[3], (MODEL_WIDTH, VALUE_WIDTH), VALUE_WIDTH ** -0.5, 0.1875, ((0, 16),)),
        "adapter_down_maps": scatter_about(part_splits[4], (MODEL_WIDTH, MEMBER_COUNT * ADAPTER_RANK), ADAPTER_RANK ** -0.5, 0.75, ((0, 16),)),
        "adapter_up_maps": scatter_about(part_splits[5], (MEMBER_COUNT * ADAPTER_RANK, VALUE_WIDTH), VALUE_WIDTH ** -0.5, 0.1875),
        "members": jnp.searchsorted(jnp.cumsum(uneven(part_splits[6], MEMBER_COUNT, BLOCKS, BLOCKS // 2, 2)), jnp.arange(BLOCKS), side="right").astype(jnp.int32),
    }


adapter_scale = 2.0


def member_mask(members, dtype):
    return (members[:, None] == jnp.arange(MEMBER_COUNT, dtype=jnp.int32)[None, :]).astype(dtype)


def expand(members, values):
    blocks = members.shape[0]
    onehot = member_mask(members, values.dtype)
    shaped = values.reshape(blocks, BLOCK, 1, ADAPTER_RANK)
    expanded_rows = shaped * onehot[:, None, :, None]
    return expanded_rows.reshape(blocks * BLOCK, MEMBER_COUNT * ADAPTER_RANK)


def member_selector(members, widened_gradient):
    blocks = members.shape[0]
    onehot = member_mask(members, widened_gradient.dtype)
    shaped = widened_gradient.reshape(blocks, BLOCK, MEMBER_COUNT, ADAPTER_RANK)
    return jnp.sum(shaped * onehot[:, None, :, None], axis=2).reshape(blocks * BLOCK, ADAPTER_RANK)


def reference(tokens, output_gradient, adapter_hidden_state, frozen_value_weight, adapter_down_maps, adapter_up_maps, members):
    widened_gradient = jnp.dot(output_gradient, adapter_up_maps.T, preferred_element_type=jnp.float32)
    adapter_gradient = (adapter_scale * member_selector(members, widened_gradient)).astype(jnp.bfloat16)
    expanded_rows = expand(members, adapter_gradient)
    adapter_contribution = lax.optimization_barrier(jnp.dot(expanded_rows, adapter_down_maps.T, preferred_element_type=jnp.float32).astype(jnp.bfloat16))
    frozen_output = jnp.dot(output_gradient, frozen_value_weight.T, preferred_element_type=jnp.float32)
    layer_input_gradient = (frozen_output + adapter_contribution.astype(jnp.float32)).astype(jnp.bfloat16)
    down_grad = jnp.dot(tokens.T, expanded_rows, preferred_element_type=jnp.float32)
    hidden_state_expanded = expand(members, adapter_hidden_state)
    up_map_gradient = adapter_scale * jnp.dot(hidden_state_expanded.T, output_gradient, preferred_element_type=jnp.float32)
    return layer_input_gradient, down_grad, up_map_gradient
```

```python
import functools

import jax
import jax.numpy as jnp
import numpy as np
from jax import lax
from jax.experimental import pallas as pl
from jax.experimental.pallas import tpu as pltpu
from jax.sharding import PartitionSpec as P

ADAPTER_RANK = 64
MEMBER_COUNT = 4
BLOCK = 128
INNER = 4

adapter_scale = 2.0

F32 = jnp.float32
BF16 = jnp.bfloat16
VMEM = pl.BlockSpec(memory_space=pltpu.VMEM)
SMEM = pl.BlockSpec(memory_space=pltpu.SMEM)
ANY = pl.BlockSpec(memory_space=pl.ANY)


def nt(a, b):
    return lax.dot_general(a, b, (((1,), (1,)), ((), ())), preferred_element_type=F32)


def tn(a, b):
    return lax.dot_general(a, b, (((0,), (0,)), ((), ())), preferred_element_type=F32)


def params(nbytes, **kw):
    return pltpu.CompilerParams(vmem_limit_bytes=nbytes, **kw)


def cost(flops, nbytes):
    return pl.CostEstimate(flops=flops, bytes_accessed=nbytes, transcendentals=0)


def where_am_i():
    me = lax.axis_index("dp")
    return me // INNER, me % INNER


def member_of_rows(members_ref, first_block, shape, dim):
    position = lax.broadcasted_iota(jnp.int32, shape, dim) // BLOCK
    result = jnp.zeros(shape, jnp.int32)
    for b in range(shape[dim] // BLOCK):
        result = jnp.where(position == b, members_ref[first_block + b], result)
    return result


def down_kernel(members, g, b, tok_send, tok_keep, send, keep, spread_t):
    rows = g.shape[0]
    width = b.shape[0]

    @pl.when(pl.program_id(0) == 0)
    def _():
        wide = nt(b[...], g[...])
        first = lax.axis_index("dp") * (rows // BLOCK)
        owner = member_of_rows(members, first, (width, rows), 1)
        column = lax.broadcasted_iota(jnp.int32, (width, rows), 0) // ADAPTER_RANK
        spread_t[...] = jnp.where(owner == column, adapter_scale * wide, 0.0).astype(BF16)

    left = spread_t[...]
    send[0] = jnp.dot(left, tok_send[...], preferred_element_type=F32).astype(BF16)
    keep[0] = jnp.dot(left, tok_keep[...], preferred_element_type=F32).astype(BF16)


def down_partials(members, g, b, tokens, per, n):
    rows, width = g.shape[0], b.shape[0]
    whole = lambda shape: pl.BlockSpec(shape, lambda i: (0, 0))
    out = pl.BlockSpec((1, width, per), lambda i: (i, 0, 0))
    shape = jax.ShapeDtypeStruct((n // 2, width, per), BF16)
    return pl.pallas_call(
        down_kernel,
        out_shape=(shape, shape),
        grid=(n // 2,),
        in_specs=[
            SMEM,
            whole(g.shape),
            whole(b.shape),
            pl.BlockSpec((rows, per), lambda i: (0, 2 * i + 1 - lax.axis_index("dp") % 2)),
            pl.BlockSpec((rows, per), lambda i: (0, 2 * i + lax.axis_index("dp") % 2)),
        ],
        out_specs=[out, out],
        scratch_shapes=[pltpu.VMEM((width, rows), BF16)],
        compiler_params=params(32 << 20),
        cost_estimate=cost(0, 0),
        name="down_partials",
    )(members, g, b, tokens, tokens)


def spread_kernel(members, b, *refs):
    gs, spread, up = refs[:INNER], refs[INNER], refs[INNER + 1]
    width, depth = b.shape
    rows = gs[0].shape[0]
    half, cols = up.shape
    z, q = where_am_i()
    total = jnp.zeros(up.shape, F32)
    for j in range(INNER):
        first = (z * INNER + (q ^ j)) * (rows // BLOCK)
        wide = nt(gs[j][:, :depth], b[...])
        owner = member_of_rows(members, first, (rows, width), 0)
        column = lax.broadcasted_iota(jnp.int32, (rows, width), 1) // ADAPTER_RANK
        spread[j] = jnp.where(owner == column, adapter_scale * wide, 0.0).astype(BF16)
        hidden = gs[j][:, depth:]
        hidden = jnp.concatenate([hidden] * (half // ADAPTER_RANK), axis=1)
        column = column[:, :half] + (q // 2) * (half // ADAPTER_RANK)
        hidden = jnp.where(owner[:, :half] == column, hidden, jnp.zeros_like(hidden))
        total = total + tn(hidden, gs[j][:, pl.ds(pl.multiple_of((q % 2) * cols, cols), cols)])
    up[...] = (adapter_scale * total).astype(BF16)


def spread_rows(members, b, gs):
    rows, (width, depth) = gs[0].shape[0], b.shape
    return pl.pallas_call(
        spread_kernel,
        out_shape=(
            jax.ShapeDtypeStruct((INNER, rows, width), BF16),
            jax.ShapeDtypeStruct((width // 2, depth // 2), BF16),
        ),
        in_specs=[SMEM] + [VMEM] * (1 + INNER),
        out_specs=[VMEM, VMEM],
        compiler_params=params(32 << 20),
        cost_estimate=cost(0, 0),
        name="spread_rows",
    )(members, b, *gs)


def multiply(gs, spread, w, a, outs, at):
    depth = w.shape[1]
    rows = gs[0].shape[0]
    for j in (2, 3, 1, 0):
        value = (nt(gs[j][:, :depth], w[...]) + nt(spread[j], a)).astype(BF16)
        if j < 2:
            outs[j][:, at] = value
        else:
            outs[2][(j - 2) * rows : (j - 1) * rows, at] = value


def own_kernel(w, a, spread, *refs):
    multiply(refs[:INNER], spread, w, a[...], refs[INNER:], slice(None))


def shard_kernel(turn, mine, theirs, a, spread, *refs):
    half = mine.shape[0]
    z, _ = where_am_i()
    parity = lax.axis_index("groups") % 2
    start = shard_of(turn, z) * (2 * half)
    for w, which in ((mine, parity), (theirs, 1 - parity)):
        at = pl.multiple_of(which * half, half)
        rows = pl.ds(pl.multiple_of(start + at, half), half)
        multiply(refs[:INNER], spread, w, a[rows, :], refs[INNER:], pl.ds(at, half))


def joined_kernel(turn, w, a, spread, *refs):
    per = w.shape[0]
    z, _ = where_am_i()
    rows = pl.ds(pl.multiple_of(shard_of(turn, z) * per, per), per)
    multiply(refs[:INNER], spread, w, a[rows, :], refs[INNER:], slice(None))


def product(kernel, per, gs, args, name):
    rows = gs[0].shape[0]
    shape = jax.ShapeDtypeStruct((rows, per), BF16)
    pair = jax.ShapeDtypeStruct((2 * rows, per), BF16)
    return pl.pallas_call(
        kernel,
        out_shape=(shape, shape, pair),
        in_specs=[VMEM] * (len(args) + INNER),
        out_specs=[VMEM] * 3,
        compiler_params=params(32 << 20),
        cost_estimate=cost(0, 0),
        name=name,
    )(*args, *gs)


def place_kernel(turn, own, core, across, both, *refs):
    out, sem = refs[-2], refs[-1]
    rows, per = own.shape
    z, q = where_am_i()
    shard = shard_of(turn, z)
    copies = []
    for j, piece in enumerate((own, core, across.at[:rows], both)):
        at = pl.ds(pl.multiple_of((shard * INNER + (q ^ j)) * per, per), per)
        copies.append(pltpu.make_async_copy(piece, out.at[:, at], sem.at[j]))
        copies[-1].start()
    for copy in copies:
        copy.wait()


def place(turn, pieces, out, shape):
    args = [*pieces] + ([out] if turn else [])
    return pl.pallas_call(
        functools.partial(place_kernel, turn),
        out_shape=shape,
        in_specs=[VMEM] * INNER + [ANY] * (len(args) - INNER),
        out_specs=ANY,
        scratch_shapes=[pltpu.SemaphoreType.DMA((INNER,))],
        input_output_aliases={len(args) - 1: 0} if turn else {},
        compiler_params=params(32 << 20),
        cost_estimate=cost(0, 0),
        name="place",
    )(*args)


def source(turn, z, planes):
    both = min(z, planes - 1 - z)
    if turn <= 2 * both:
        return (turn + 1) // 2, 1 - turn % 2
    even_is_far = (z % 2 == 0) == (z < planes // 2)
    return turn - both, 0 if even_is_far else 1


def far_plane(z, step, link):
    return z + step if z % 2 == link else z - step


def shard_of(turn, z):
    planes = lax.axis_size("dp") // INNER
    result = z
    if turn:
        for plane in range(planes):
            step, link = source(turn, plane, planes)
            result = jnp.where(z == plane, far_plane(plane, step, link), result)
    return result


def edges(step, link, planes):
    pairs = []
    for z in range(planes):
        right = z % 2 == link
        origin, to = (z - step + 1, z + 1) if right else (z + step - 1, z - 1)
        if 0 <= origin < planes and 0 <= to < planes:
            pairs.append((z, to))
    return pairs


def local(tokens, output_gradient, hidden, frozen, down_maps, up_maps, members):
    n = lax.axis_size("dp")
    groups = lax.axis_size("groups")
    planes = n // INNER
    me = lax.axis_index("dp")
    z, q = me // INNER, me % INNER
    parity = lax.axis_index("groups") % 2
    per = frozen.shape[0]
    width, depth = up_maps.shape

    def inner(x, bit):
        return lax.ppermute(x, "dp", [(i, i ^ bit) for i in range(n)])

    def along(x, pairs):
        return lax.ppermute(
            x, "dp", [(s * INNER + i, t * INNER + i) for s, t in pairs for i in range(INNER)]
        )

    def twin(x):
        return lax.ppermute(x, "groups", [(i, i ^ 1) for i in range(groups)])

    maps = lax.all_gather(
        down_maps,
        "dp",
        axis=0,
        tiled=True,
        axis_index_groups=[[p * INNER + i for p in range(planes)] for i in range(INNER)],
    )
    half = per // 2
    part = lax.dynamic_slice_in_dim(frozen, parity * half, half)
    packed = jnp.concatenate([output_gradient, hidden], axis=1)
    g2 = inner(packed, 2)
    held = {(0, 0): part, (0, 1): part}
    for k in range(1, planes):
        for link in (0, 1):
            pairs = edges(k, link, planes)
            if pairs:
                held[k, link] = along(held[k - 1, 1 - link], pairs)

    g1 = inner(packed, 1)
    g3 = inner(g2, 1)
    gs = [packed, g1, g2, g3]

    send, keep = down_partials(members, output_gradient, up_maps, tokens, per, n)
    got = inner(send, 1)
    spread, up = spread_rows(members, up_maps, gs)

    out_shape = jax.ShapeDtypeStruct(tokens.shape, BF16)
    rows = tokens.shape[0]

    def exchange(own, sibling, pair):
        across = inner(pair, 2)
        return own, inner(sibling, 1), across, inner(across[rows:], 1)

    blocks = product(own_kernel, per, gs, (frozen, down_maps, spread), "own_shard")
    result = place(0, exchange(*blocks), None, out_shape)
    for turn in range(1, planes):
        where = [source(turn, p, planes) for p in range(planes)]
        mine = held[where[0]]
        for option in sorted(set(where) - {where[0]}):
            hit = functools.reduce(
                jnp.logical_or, [z == p for p in range(planes) if where[p] == option]
            )
            mine = jnp.where(hit, held[option], mine)
        theirs = twin(mine)
        if half % 128:
            low, high = jnp.where(parity == 0, mine, theirs), jnp.where(parity == 0, theirs, mine)
            args = (jnp.concatenate([low, high]), maps, spread)
            kernel = functools.partial(joined_kernel, turn)
        else:
            args = (mine, theirs, maps, spread)
            kernel = functools.partial(shard_kernel, turn)
        blocks = product(kernel, per, gs, args, "shard")
        result = place(turn, exchange(*blocks), result, out_shape)

    keep = keep.reshape(planes, 2 * width, per)
    got = got.reshape(planes, 2 * width, per)
    up = up.reshape(planes, up.size // planes // per, per)

    def term(t):
        t = jnp.clip(t, 0, planes - 1)
        down = lax.dynamic_index_in_dim(keep, t, keepdims=False).astype(F32)
        down = down + lax.dynamic_index_in_dim(got, t, keepdims=False).astype(F32)
        return jnp.concatenate([down, lax.dynamic_index_in_dim(up, t, keepdims=False).astype(F32)])

    came = {}
    for k in range(planes - 1, 0, -1):
        for link in (0, 1):
            pairs = [(t, s) for s, t in edges(k, link, planes)]
            if pairs:
                value = term(jnp.where(z % 2 == link, z + k, z - k))
                if (k + 1, 1 - link) in came:
                    value = value + came[k + 1, 1 - link].astype(F32)
                came[k, link] = along(value.astype(BF16), pairs)
    total = term(z)
    for link in (0, 1):
        if (1, link) in came:
            total = total + came[1, link].astype(F32)
    y = q // 2
    down = total[: 2 * width].reshape(2, width, per)
    other = inner(lax.dynamic_index_in_dim(down, 1 - y, keepdims=False).astype(BF16), 2)
    down = lax.dynamic_index_in_dim(down, y, keepdims=False) + other.astype(F32)
    down_grad = down.T

    piece = total[2 * width :].astype(BF16)
    pieces = jnp.zeros((planes,) + piece.shape, BF16)
    pieces = lax.dynamic_update_index_in_dim(pieces, piece, z, 0)
    for k in range(1, planes):
        moved = along(piece, [(s, (s + k) % planes) for s in range(planes)])
        pieces = lax.dynamic_update_index_in_dim(pieces, moved, (z - k) % planes, 0)
    mine = pieces.reshape(width // 2, depth // 2)
    theirs = inner(mine, 2)
    mine = jnp.concatenate([jnp.where(y == 0, mine, theirs), jnp.where(y == 0, theirs, mine)])
    theirs = inner(mine, 1)
    c = q % 2
    up_grad = jnp.concatenate(
        [jnp.where(c == 0, mine, theirs), jnp.where(c == 0, theirs, mine)], axis=1
    ).astype(F32)
    return result, down_grad, up_grad


def solution(mesh):
    in_specs = (
        P(("groups", "dp"), None),
        P(("groups", "dp"), None),
        P(("groups", "dp"), None),
        P("dp", None),
        P(("groups", "dp"), None),
        P("groups", None),
        P("groups"),
    )
    out_specs = (P(("groups", "dp"), None), P(("groups", "dp"), None), P("groups", None))
    return jax.shard_map(local, mesh=mesh, in_specs=in_specs, out_specs=out_specs, check_vma=False)
```

```python
import functools

import jax
import jax.numpy as jnp
import numpy as np
from jax import lax
from jax.experimental import pallas as pl
from jax.experimental.pallas import tpu as pltpu
from jax.sharding import PartitionSpec as P

ADAPTER_RANK = 64
MEMBER_COUNT = 4
BLOCK = 128
HIDDEN_COPIES = 2
INNER = 4

adapter_scale = 2.0
VMEM_BYTES = 24 << 20

COST_DOWN = 6
COST_SPREAD = 40
COST_MM = 3
COST_PLACE = 1
COST_LAST = 15
COST_OWN = 40
COST_TERM = 4

F32 = jnp.float32
BF16 = jnp.bfloat16
VMEM = pl.BlockSpec(memory_space=pltpu.VMEM)
SMEM = pl.BlockSpec(memory_space=pltpu.SMEM)
ANY = pl.BlockSpec(memory_space=pl.ANY)
HBM = pl.BlockSpec(memory_space=pltpu.HBM)


def nt(a, b):
    return lax.dot_general(a, b, (((1,), (1,)), ((), ())), preferred_element_type=F32)


def tn(a, b):
    return lax.dot_general(a, b, (((0,), (0,)), ((), ())), preferred_element_type=F32)


def params(nbytes, **kw):
    return pltpu.CompilerParams(vmem_limit_bytes=nbytes, **kw)


def cost(microseconds):
    return pl.CostEstimate(
        flops=int(microseconds * 1.1e9), bytes_accessed=int(microseconds * 3.3e6), transcendentals=0
    )


def where_am_i():
    me = lax.axis_index("dp")
    return me // INNER, me % INNER


def member_of_rows(members_ref, first_block, shape, dim):
    position = lax.broadcasted_iota(jnp.int32, shape, dim) // BLOCK
    result = jnp.zeros(shape, jnp.int32)
    for b in range(shape[dim] // BLOCK):
        result = jnp.where(position == b, members_ref[first_block + b], result)
    return result


def first_kernel(split, frozen, maps, g, h, part, packed, h_in, h_out, sems):
    half, depth = frozen.shape[0] // split, frozen.shape[1]
    width = maps.shape[1]
    at = pl.multiple_of(lax.axis_index("groups") % split * half, half)
    load = pltpu.make_async_copy(h, h_in, sems.at[0])
    copies = [
        pltpu.make_async_copy(g, packed.at[:, :depth], sems.at[1]),
        pltpu.make_async_copy(frozen.at[pl.ds(at, half)], part.at[:, :depth], sems.at[2]),
    ]
    for i in range(split):
        cols = slice(depth + i * width, depth + (i + 1) * width)
        rows = slice(i * half, (i + 1) * half)
        copies.append(pltpu.make_async_copy(maps.at[rows], part.at[:, cols], sems.at[3 + i]))
    load.start()
    for copy in copies:
        copy.start()
    load.wait()
    h_out[...] = jnp.concatenate([h_in[...].T] * HIDDEN_COPIES, axis=1)
    copies.append(pltpu.make_async_copy(h_out, packed.at[:, depth:], sems.at[5]))
    copies[-1].start()
    for copy in copies:
        copy.wait()


def first_sent(split, frozen, maps, g, h):
    half, depth = frozen.shape[0] // split, frozen.shape[1]
    rows = g.shape[0]
    part = (half, depth + split * maps.shape[1])
    packed = (rows, depth + HIDDEN_COPIES * ADAPTER_RANK)
    return pl.pallas_call(
        functools.partial(first_kernel, split),
        out_shape=(jax.ShapeDtypeStruct(part, BF16), jax.ShapeDtypeStruct(packed, BF16)),
        in_specs=[HBM] * 4,
        out_specs=[ANY, ANY],
        scratch_shapes=[
            pltpu.VMEM(h.shape, BF16),
            pltpu.VMEM((rows, HIDDEN_COPIES * ADAPTER_RANK), BF16),
            pltpu.SemaphoreType.DMA((6,)),
        ],
        compiler_params=params(8 << 20),
        cost_estimate=cost(1),
        name="first_sent",
    )(frozen, maps, g, h)


def hold_kernel(*refs):
    del refs


def hold(x, *after):
    return pl.pallas_call(
        hold_kernel,
        out_shape=jax.ShapeDtypeStruct(x.shape, x.dtype),
        in_specs=[ANY] * (1 + len(after)),
        out_specs=ANY,
        input_output_aliases={0: 0},
        compiler_params=params(1 << 20),
        cost_estimate=cost(0),
        name="hold",
    )(x, *after)


def down_kernel(members, g, b, tokens, after, send, keep, g_in, b_in, block, result, sems, out_sems):
    del after
    rows, width = g.shape[0], b.shape[0]
    blocks, _, per = send.shape
    me = lax.axis_index("dp")
    first = [
        pltpu.make_async_copy(g, g_in, out_sems.at[0]),
        pltpu.make_async_copy(b, b_in, out_sems.at[1]),
    ]
    loads = []
    for i in range(2 * blocks):
        mine = me % 2 if i % 2 else 1 - me % 2
        at = pl.ds(pl.multiple_of((i // 2 * 2 + mine) * per, per), per)
        loads.append(pltpu.make_async_copy(tokens.at[:, at], block.at[i], sems.at[i]))
    for copy in first + loads:
        copy.start()
    for copy in first:
        copy.wait()
    wide = nt(b_in[...], g_in[...])
    owner = member_of_rows(members, me * (rows // BLOCK), (width, rows), 1)
    column = lax.broadcasted_iota(jnp.int32, (width, rows), 0) // ADAPTER_RANK
    left = jnp.where(owner == column, adapter_scale * wide, 0.0).astype(BF16)
    stores = []
    for i in [*range(0, 2 * blocks, 2), *range(1, 2 * blocks, 2)]:
        loads[i].wait()
        result[i] = jnp.dot(left, block[i], preferred_element_type=F32).astype(BF16)
        target = (keep if i % 2 else send).at[i // 2]
        stores.append(pltpu.make_async_copy(result.at[i], target, out_sems.at[2 + i]))
        stores[-1].start()
    for copy in stores:
        copy.wait()


def down_partials(members, g, b, tokens, per, n, after):
    rows, width = g.shape[0], b.shape[0]
    shape = jax.ShapeDtypeStruct((n // 2, width, per), BF16)
    return pl.pallas_call(
        down_kernel,
        out_shape=(shape, shape),
        in_specs=[SMEM] + [HBM] * 3 + [ANY],
        out_specs=[ANY, ANY],
        scratch_shapes=[
            pltpu.VMEM(g.shape, BF16),
            pltpu.VMEM(b.shape, BF16),
            pltpu.VMEM((n, rows, per), BF16),
            pltpu.VMEM((n, width, per), BF16),
            pltpu.SemaphoreType.DMA((n,)),
            pltpu.SemaphoreType.DMA((n + 2,)),
        ],
        compiler_params=params(12 << 20),
        cost_estimate=cost(COST_DOWN),
        name="down_partials",
    )(members, g, b, tokens, after)


def spread_kernel(members, b, *refs):
    gs, spread, up = refs[:INNER], refs[INNER], refs[INNER + 1]
    width, depth = b.shape
    rows = gs[0].shape[0]
    planes, piece, per = up.shape
    half, cols = width // 2, depth // 2
    across = cols // per
    z, q = where_am_i()
    total = jnp.zeros((half, cols), F32)
    for j in range(INNER):
        first = (z * INNER + (q ^ j)) * (rows // BLOCK)
        wide = nt(gs[j][:, :depth], b[...])
        owner = member_of_rows(members, first, (rows, width), 0)
        column = lax.broadcasted_iota(jnp.int32, (rows, width), 1) // ADAPTER_RANK
        spread[j] = jnp.where(owner == column, adapter_scale * wide, 0.0).astype(BF16)
        hidden = gs[j][:, depth:]
        column = column[:, :half] + (q // 2) * (half // ADAPTER_RANK)
        hidden = jnp.where(owner[:, :half] == column, hidden, jnp.zeros_like(hidden))
        total = total + tn(hidden, gs[j][:, pl.ds(pl.multiple_of((q % 2) * cols, cols), cols)])
    total = (adapter_scale * total).astype(BF16)
    for t in range(planes):
        row, col = t // across * piece, t % across * per
        up[t] = total[row : row + piece, col : col + per]


def spread_rows(members, b, gs, per, planes):
    rows, (width, depth) = gs[0].shape[0], b.shape
    return pl.pallas_call(
        spread_kernel,
        out_shape=(
            jax.ShapeDtypeStruct((INNER, rows, width), BF16),
            jax.ShapeDtypeStruct((planes, width * depth // (INNER * planes * per), per), BF16),
        ),
        in_specs=[SMEM] + [VMEM] * (1 + INNER),
        out_specs=[VMEM, VMEM],
        compiler_params=params(8 << 20),
        cost_estimate=cost(COST_SPREAD),
        name="spread_rows",
    )(members, b, *gs)


def on_choice(turn, options, act):
    planes = lax.axis_size("dp") // INNER
    z, _ = where_am_i()
    for i, option in enumerate(options):
        hit = functools.reduce(
            jnp.logical_or,
            [z == p for p in range(planes) if source(turn, p, planes) == option],
        )
        pl.when(hit)(functools.partial(act, i))


def part_index(side):
    if side in (0, 1):
        return side
    parity = lax.axis_index("groups") % 2
    return parity if side == "mine" else 1 - parity


def product_kernel(plan, n_sources, *refs):
    spread, gs, refs = refs[0], refs[1 : 1 + INNER], refs[1 + INNER :]
    sources, outs, (a, sems) = refs[:n_sources], refs[-5:-2], refs[-2:]
    _, unit, width = a.shape
    rows = gs[0].shape[0]
    weights, copies = [], []
    for h, (turn, side, split, w_at, maps_at) in enumerate(plan):
        index = part_index(side) if split > 1 else 0
        if turn:
            weights.append(sources[w_at])
            depth = sources[w_at].shape[1]
            cols = pl.ds(pl.multiple_of(depth + index * width, width), width)

            def maps(i, h=h, cols=cols, maps_at=maps_at):
                return pltpu.make_async_copy(
                    sources[maps_at[i][1]].at[:, cols], a.at[h], sems.at[h]
                )

            on_choice(turn, [o for o, _ in maps_at], lambda i, maps=maps: maps(i).start())
            copies.append(maps(0))
        else:
            at = slice(index * unit, (index + 1) * unit)
            weights.append(sources[w_at].at[at])
            copies.append(pltpu.make_async_copy(sources[maps_at].at[at], a.at[h], sems.at[h]))
            copies[-1].start()
    for copy in copies:
        copy.wait()
    for j in (2, 3, 1, 0):
        for h, w in enumerate(weights):
            value = (nt(gs[j][:, : w.shape[1]], w[...]) + nt(spread[j], a[h])).astype(BF16)
            at = slice(h * unit, (h + 1) * unit)
            if j < 2:
                outs[j][:, at] = value
            else:
                outs[2][(j - 2) * rows : (j - 1) * rows, at] = value


def product(plan, sources, spread, gs, unit, after):
    rows, width = gs[0].shape[0], spread.shape[2]
    n, cols = len(plan), len(plan) * unit
    shape = jax.ShapeDtypeStruct((rows, cols), BF16)
    pair = jax.ShapeDtypeStruct((2 * rows, cols), BF16)
    weights = {w_at for _, _, _, w_at, _ in plan}
    return pl.pallas_call(
        functools.partial(product_kernel, plan, len(sources)),
        out_shape=(shape, shape, pair),
        in_specs=[VMEM] * (1 + INNER)
        + [VMEM if i in weights else ANY for i in range(len(sources))]
        + [ANY] * len(after),
        out_specs=[VMEM] * 3,
        scratch_shapes=[pltpu.VMEM((n, unit, width), BF16), pltpu.SemaphoreType.DMA((n,))],
        compiler_params=params(12 << 20),
        cost_estimate=cost(COST_MM),
        name="product",
    )(spread, *gs, *sources, *after)


def choose_kernel(turn, options, *refs):
    out, sem = refs[-2], refs[-1]
    depth = out.shape[1]

    def fetch(i):
        copy = pltpu.make_async_copy(refs[i].at[:, :depth], out, sem)
        copy.start()
        copy.wait()

    on_choice(turn, options, fetch)


def choose(turn, options, parts, depth, after):
    half = parts[0].shape[0]
    return pl.pallas_call(
        functools.partial(choose_kernel, turn, options),
        out_shape=jax.ShapeDtypeStruct((half, depth), BF16),
        in_specs=[ANY] * (len(parts) + len(after)),
        out_specs=VMEM,
        scratch_shapes=[pltpu.SemaphoreType.DMA],
        compiler_params=params(4 << 20),
        cost_estimate=cost(1),
        name="choose",
    )(*parts, *after)


def place_kernel(plan, own, core, across, both, *refs):
    out, token, sem = refs[-3:]
    rows, cols = own.shape
    unit = cols // len(plan)
    z, q = where_am_i()
    copies = []
    for h, (turn, side, split, *_) in enumerate(plan):
        index = part_index(side) if split > 1 else 0
        shard = shard_of(turn, z) * INNER
        for j, piece in enumerate((own, core, across, both)):
            at = pl.ds(pl.multiple_of(((shard + (q ^ j)) * split + index) * unit, unit), unit)
            source = piece.at[:rows, h * unit : (h + 1) * unit]
            copies.append(pltpu.make_async_copy(source, out.at[:, at], sem.at[h, j]))
            copies[-1].start()
    token[...] = jnp.zeros(token.shape, F32)
    for copy in copies:
        copy.wait()


def place(plan, pieces, out, shape, after, microseconds=COST_PLACE):
    given = [] if out is None else [out]
    return pl.pallas_call(
        functools.partial(place_kernel, plan),
        out_shape=(shape, jax.ShapeDtypeStruct((8, 128), F32)),
        in_specs=[VMEM] * INNER + [ANY] * (len(given) + len(after)),
        out_specs=[ANY, VMEM],
        scratch_shapes=[pltpu.SemaphoreType.DMA((len(plan), INNER))],
        input_output_aliases={INNER: 0} if given else {},
        compiler_params=params(6 << 20),
        cost_estimate=cost(microseconds),
        name="place",
    )(*pieces, *given, *after)


def start_loads(keep, got, up, came, t, block, sems):
    width = keep.shape[1]
    copies = [
        pltpu.make_async_copy(keep.at[2 * t + i], block.at[0, i * width : (i + 1) * width], sems.at[i])
        for i in range(2)
    ] + [
        pltpu.make_async_copy(got.at[2 * t + i], block.at[1, i * width : (i + 1) * width], sems.at[2 + i])
        for i in range(2)
    ]
    copies.append(pltpu.make_async_copy(up.at[t], block.at[0, 2 * width :], sems.at[4]))
    for i, c in enumerate(came):
        copies.append(pltpu.make_async_copy(c, block.at[2 + i], sems.at[5 + i]))
    for copy in copies:
        copy.start()
    return copies


def add_up(block, width, n_came):
    values = []
    for at in (slice(0, width), slice(width, 2 * width), slice(2 * width, None)):
        value = block[0, at].astype(F32)
        if at.stop:
            value = value + block[1, at].astype(F32)
        for i in range(n_came):
            value = value + block[2 + i, at].astype(F32)
        values.append(value)
    return values


def term_kernel(step, links, n_came, *refs):
    came, (keep, got, up), refs = refs[:n_came], refs[n_came : n_came + 3], refs[n_came + 3 :]
    n = len(links)
    width = keep.shape[1]
    outs, block, sems = refs[-2 - n : -2], refs[-2], refs[-1]
    planes = lax.axis_size("dp") // INNER
    z, _ = where_am_i()
    given, loads = list(came), []
    for i, (link, has) in enumerate(links):
        t = jnp.clip(jnp.where(z % 2 == link, z + step, z - step), 0, planes - 1)
        before = [given.pop(0)] if has else []
        loads.append(start_loads(keep, got, up, before, t, block.at[i], sems.at[i]))
    for i, (link, has) in enumerate(links):
        for copy in loads[i]:
            copy.wait()
        first, second, value = add_up(block.at[i], width, 1 if has else 0)
        outs[i][:width] = first.astype(BF16)
        outs[i][width : 2 * width] = second.astype(BF16)
        outs[i][2 * width :] = value.astype(BF16)


def terms(step, links, came, keep, got, up, after):
    rows = 2 * keep.shape[1] + up.shape[1]
    shape = jax.ShapeDtypeStruct((rows, keep.shape[2]), BF16)
    return pl.pallas_call(
        functools.partial(term_kernel, step, links, len(came)),
        out_shape=(shape,) * len(links),
        in_specs=[ANY] * (len(came) + 3 + len(after)),
        out_specs=[VMEM] * len(links),
        scratch_shapes=[
            pltpu.VMEM((len(links), 3, *shape.shape), BF16),
            pltpu.SemaphoreType.DMA((len(links), 6)),
        ],
        compiler_params=params(10 << 20),
        cost_estimate=cost(COST_TERM),
        name="running_sums",
    )(*came, keep, got, up, *after)


def total_kernel(n_came, *refs):
    came, (keep, got, up), refs = refs[:n_came], refs[n_came : n_came + 3], refs[n_came + 3 :]
    send, kept, piece, block, sems = refs[-5:]
    z, q = where_am_i()
    for copy in start_loads(keep, got, up, came, z, block, sems):
        copy.wait()
    first, second, value = add_up(block, keep.shape[1], n_came)
    low = q // 2 == 0
    kept[...] = jnp.where(low, first, second)
    send[...] = jnp.where(low, second, first).astype(BF16)
    piece[...] = value.astype(BF16)


def totals(came, keep, got, up, after):
    rows = 2 * keep.shape[1] + up.shape[1]
    return pl.pallas_call(
        functools.partial(total_kernel, len(came)),
        out_shape=(
            jax.ShapeDtypeStruct(keep.shape[1:], BF16),
            jax.ShapeDtypeStruct(keep.shape[1:], F32),
            jax.ShapeDtypeStruct(up.shape[1:], BF16),
        ),
        in_specs=[ANY] * (len(came) + 3 + len(after)),
        out_specs=[VMEM] * 3,
        scratch_shapes=[
            pltpu.VMEM((2 + len(came), rows, keep.shape[2]), BF16),
            pltpu.SemaphoreType.DMA((5 + len(came),)),
        ],
        compiler_params=params(10 << 20),
        cost_estimate=cost(COST_TERM),
        name="totals",
    )(*came, keep, got, up, *after)


def quarter_kernel(*refs):
    pieces, out = refs[:-1], refs[-1]
    planes = len(pieces)
    rows, per = pieces[0].shape
    across = out.shape[1] // per
    z, _ = where_am_i()
    for k, piece in enumerate(pieces):
        t = (z - k + planes) % planes
        row = pl.ds(pl.multiple_of(t // across * rows, rows), rows)
        col = pl.ds(pl.multiple_of(t % across * per, per), per)
        out[row, col] = piece[...]


def quarter(pieces, shape):
    return pl.pallas_call(
        quarter_kernel,
        out_shape=jax.ShapeDtypeStruct(shape, BF16),
        in_specs=[VMEM] * len(pieces),
        out_specs=VMEM,
        compiler_params=params(2 << 20),
        cost_estimate=cost(1),
        name="quarter",
    )(*pieces)


def finish_kernel(kept, other, q0, q1, q2, q3, down, up):
    down[...] = (kept[...] + other[...].astype(F32)).T
    rows, cols = q0.shape
    _, q = where_am_i()
    for j, part in enumerate((q0, q1, q2, q3)):
        row = pl.ds(pl.multiple_of((q ^ j) // 2 * rows, rows), rows)
        col = pl.ds(pl.multiple_of((q ^ j) % 2 * cols, cols), cols)
        up[row, col] = part[...].astype(F32)


def finish(kept, other, quarters):
    rows, cols = quarters[0].shape
    return pl.pallas_call(
        finish_kernel,
        out_shape=(
            jax.ShapeDtypeStruct(kept.shape[::-1], F32),
            jax.ShapeDtypeStruct((2 * rows, 2 * cols), F32),
        ),
        in_specs=[VMEM] * 6,
        out_specs=[VMEM] * 2,
        compiler_params=params(6 << 20),
        cost_estimate=cost(1),
        name="finish",
    )(kept, other, *quarters)


def source(turn, z, planes):
    both = min(z, planes - 1 - z)
    if turn <= 2 * both:
        return (turn + 1) // 2, 1 - turn % 2
    even_is_far = (z % 2 == 0) == (z < planes // 2)
    return turn - both, 0 if even_is_far else 1


def far_plane(z, step, link):
    return z + step if z % 2 == link else z - step


def shard_of(turn, z):
    planes = lax.axis_size("dp") // INNER
    result = z
    if turn:
        for plane in range(planes):
            step, link = source(turn, plane, planes)
            result = jnp.where(z == plane, far_plane(plane, step, link), result)
    return result


def edges(step, link, planes):
    pairs = []
    for z in range(planes):
        right = z % 2 == link
        origin, to = (z - step + 1, z + 1) if right else (z + step - 1, z - 1)
        if 0 <= origin < planes and 0 <= to < planes:
            pairs.append((z, to))
    return pairs


def local(tokens, output_gradient, hidden, frozen, down_maps, up_maps, members):
    n = lax.axis_size("dp")
    groups = lax.axis_size("groups")
    planes = n // INNER
    per = frozen.shape[0]
    rows = tokens.shape[0]
    width, depth = up_maps.shape
    split = 2 if per % 256 == 0 and groups % 2 == 0 else 1
    unit = per // split

    def inner(x, bit):
        return lax.ppermute(x, "dp", [(i, i ^ bit) for i in range(n)])

    def along(x, pairs):
        return lax.ppermute(
            x, "dp", [(s * INNER + i, t * INNER + i) for s, t in pairs for i in range(INNER)]
        )

    def twin(x):
        return lax.ppermute(x, "groups", [(i, i ^ 1) for i in range(groups)])

    held = {}

    def pass_on(k):
        for link in (0, 1):
            if k > 1 and (k - 1, link) in held:
                held[k - 1, link] = hold(held[k - 1, link], mine[k - 1])
        for link in (0, 1):
            pairs = edges(k, link, planes) if k < planes else []
            if pairs:
                held[k, link] = along(held[k - 1, 1 - link], pairs)

    came = {}

    def add_on(k, after):
        links = [l for l in (0, 1) if edges(k, l, planes)]
        got_before = [came[k + 1, 1 - l] for l in links if (k + 1, 1 - l) in came]
        flags = [(l, (k + 1, 1 - l) in came) for l in links]
        values = terms(k, flags, got_before, keep, got, up, after)
        for link, value in zip(links, values):
            came[k, link] = along(value, [(t, s) for s, t in edges(k, link, planes)])
        return values[0]

    at = lax.axis_index("groups") % split * unit
    maps = [down_maps[i * unit : (i + 1) * unit] for i in range(split)]
    part = jnp.concatenate([lax.dynamic_slice_in_dim(frozen, at, unit), *maps], axis=1)
    packed = jnp.concatenate([output_gradient] + [hidden] * HIDDEN_COPIES, axis=1)
    held[0, 0] = held[0, 1] = part
    g2 = inner(packed, 2)
    pass_on(1)
    g1 = inner(packed, 1)
    send, keep = down_partials(members, output_gradient, up_maps, tokens, per, n, g1)
    got = inner(send, 1)
    g2 = hold(g2, send)
    g3 = inner(g2, 1)
    gs = [packed, g1, g2, g3]
    spread, up = spread_rows(members, up_maps, gs, per, planes)

    out_shape = jax.ShapeDtypeStruct(tokens.shape, BF16)

    def hand_on(turn, after):
        own, core, across = pieces[turn]
        if after is not None:
            across = hold(across, after)
        pieces[turn] = own, core, across, inner(across[rows:], 1)

    mine, theirs, plans, pieces = {}, {}, {}, {}
    result, token = None, send

    def shard_options(turn):
        options = sorted({source(turn, p, planes) for p in range(planes)})
        return options, [held[o] for o in options]

    def multiply(k, after):
        sources, plan = [], []

        def add(x):
            sources.append(x)
            return len(sources) - 1

        def add_part(turn, side, w):
            options, parts = shard_options(turn)
            maps = [(option, add(x)) for option, x in zip(options, parts)]
            plan.append((turn, side, split, add(w), maps))

        if k == 1:
            at = add(frozen), add(down_maps)
            plan += [(0, i, split, *at) for i in range(split)]
        elif split > 1:
            add_part(k - 1, "theirs", theirs[k - 1])
        if k < planes:
            add_part(k, "mine", mine[k])
        if not plan:
            return after[0]
        plans[k] = plan
        blocks = product(plan, sources, spread, gs, unit, after)
        pieces[k] = blocks[0], inner(blocks[1], 1), inner(blocks[2], 2)
        return blocks[0]

    def hand_on(k, after):
        own, core, across = pieces[k]
        if after is not None:
            across = hold(across, after)
        pieces[k] = own, core, across, inner(across[rows:], 1)
        return across

    last = send
    for k in range(1, planes):
        options, parts = shard_options(k)
        waits = [held[k, l] for l in (0, 1) if (k, l) in held]
        waits += [theirs[k - 1]] if k - 1 in theirs else []
        waits += [came[planes - k + 1, l] for l in (0, 1) if (planes - k + 1, l) in came]
        mine[k] = choose(k, options, parts, depth, waits + [last, token])
        pass_on(k + 1)
        if split > 1:
            theirs[k] = twin(mine[k])
        summed = add_on(planes - k, [mine[k]])
        across = hand_on(k - 1, summed) if k > 1 else summed
        last = multiply(k, [across])
        if k > 1:
            result, token = place(plans[k - 1], pieces[k - 1], result, out_shape, [last])
    if planes > 1:
        last = hand_on(planes - 1, last)
    last = multiply(planes, [last])
    if planes > 1:
        result, token = place(plans[planes - 1], pieces[planes - 1], result, out_shape, [last])
    came_last = [came[1, l] for l in (0, 1) if (1, l) in came]
    down_send, down_kept, piece = totals(came_last, keep, got, up, [])
    other = inner(down_send, 2)
    moved = [
        along(piece, [(s, (s + k) % planes) for s in range(planes)]) for k in range(1, planes)
    ]
    mine_up = quarter([piece, *moved], (width // 2, depth // 2))
    over_y = inner(mine_up, 2)
    quarters = [mine_up, inner(mine_up, 1), over_y, inner(over_y, 1)]
    if planes in plans:
        hand_on(planes, None)
        result, token = place(plans[planes], pieces[planes], result, out_shape, [], COST_LAST)
    down_grad, up_grad = finish(down_kept, other, quarters)
    return result, down_grad, up_grad


def solution(mesh):
    in_specs = (
        P(("groups", "dp"), None),
        P(("groups", "dp"), None),
        P(("groups", "dp"), None),
        P("dp", None),
        P(("groups", "dp"), None),
        P("groups", None),
        P("groups"),
    )
    out_specs = (P(("groups", "dp"), None), P(("groups", "dp"), None), P("groups", None))
    return jax.shard_map(local, mesh=mesh, in_specs=in_specs, out_specs=out_specs, check_vma=False)
```

```python
import functools

import jax
import jax.numpy as jnp
import numpy as np
from jax import lax
from jax.experimental import pallas as pl
from jax.experimental.pallas import tpu as pltpu
from jax.sharding import PartitionSpec as P

ADAPTER_RANK = 64
MEMBER_COUNT = 4
BLOCK = 128
HIDDEN_COPIES = 2
INNER = 4

adapter_scale = 2.0
VMEM_BYTES = 24 << 20

COST_DOWN = 1
COST_SPREAD = 2.0
COST_CHOOSE = 40.0
COST_MM = 3.0
COST_PLACE = 1.0
COST_HAND = 30
COST_DOWN_END = 10.0
COST_TWIN = 10.0
COST_LAST = 10
COST_OWN = 40
COST_TERM = 4.0

F32 = jnp.float32
BF16 = jnp.bfloat16
VMEM = pl.BlockSpec(memory_space=pltpu.VMEM)
SMEM = pl.BlockSpec(memory_space=pltpu.SMEM)
ANY = pl.BlockSpec(memory_space=pl.ANY)
HBM = pl.BlockSpec(memory_space=pltpu.HBM)


def nt(a, b):
    return lax.dot_general(a, b, (((1,), (1,)), ((), ())), preferred_element_type=F32)


def tn(a, b):
    return lax.dot_general(a, b, (((0,), (0,)), ((), ())), preferred_element_type=F32)


def params(nbytes, **kw):
    return pltpu.CompilerParams(vmem_limit_bytes=nbytes, **kw)


def cost(microseconds):
    return pl.CostEstimate(
        flops=int(microseconds * 1.1e9), bytes_accessed=int(microseconds * 3.3e6), transcendentals=0
    )


def where_am_i():
    me = lax.axis_index("dp")
    return me // INNER, me % INNER


def member_of_rows(members_ref, first_block, shape, dim):
    position = lax.broadcasted_iota(jnp.int32, shape, dim) // BLOCK
    result = jnp.zeros(shape, jnp.int32)
    for b in range(shape[dim] // BLOCK):
        result = jnp.where(position == b, members_ref[first_block + b], result)
    return result


def hidden_kernel(h, after, out):
    del after
    out[...] = jnp.concatenate([h[...].T] * HIDDEN_COPIES, axis=1)


def hidden_pair(h, after):
    return pl.pallas_call(
        hidden_kernel,
        out_shape=jax.ShapeDtypeStruct((h.shape[1], HIDDEN_COPIES * h.shape[0]), BF16),
        in_specs=[VMEM, ANY],
        out_specs=VMEM,
        compiler_params=params(2 << 20),
        cost_estimate=cost(0.1),
        name="hidden_pair",
    )(h, after)


def hold_kernel(*refs):
    del refs


def hold(x, *after, microseconds=0):
    return pl.pallas_call(
        hold_kernel,
        out_shape=jax.ShapeDtypeStruct(x.shape, x.dtype),
        in_specs=[ANY] * (1 + len(after)),
        out_specs=ANY,
        input_output_aliases={0: 0},
        compiler_params=params(1 << 20),
        cost_estimate=cost(microseconds),
        name="hold",
    )(x, *after)


def down_kernel(members, g, b, tokens, after, send, keep, g_in, b_in, block, result, sems, out_sems):
    del after
    rows, width = g.shape[0], b.shape[0]
    blocks, _, per = send.shape
    me = lax.axis_index("dp")
    first = [
        pltpu.make_async_copy(g, g_in, out_sems.at[0]),
        pltpu.make_async_copy(b, b_in, out_sems.at[1]),
    ]
    loads = []
    for i in range(2 * blocks):
        mine = me % 2 if i % 2 else 1 - me % 2
        at = pl.ds(pl.multiple_of((i // 2 * 2 + mine) * per, per), per)
        loads.append(pltpu.make_async_copy(tokens.at[:, at], block.at[i], sems.at[i]))
    for copy in first + loads:
        copy.start()
    for copy in first:
        copy.wait()
    wide = nt(b_in[...], g_in[...])
    owner = member_of_rows(members, me * (rows // BLOCK), (width, rows), 1)
    column = lax.broadcasted_iota(jnp.int32, (width, rows), 0) // ADAPTER_RANK
    left = jnp.where(owner == column, adapter_scale * wide, 0.0).astype(BF16)
    stores = []
    for i in [*range(0, 2 * blocks, 2), *range(1, 2 * blocks, 2)]:
        loads[i].wait()
        result[i] = jnp.dot(left, block[i], preferred_element_type=F32).astype(BF16)
        target = (keep if i % 2 else send).at[i // 2]
        stores.append(pltpu.make_async_copy(result.at[i], target, out_sems.at[2 + i]))
        stores[-1].start()
    for copy in stores:
        copy.wait()


def down_partials(members, g, b, tokens, per, n, after):
    rows, width = g.shape[0], b.shape[0]
    shape = jax.ShapeDtypeStruct((n // 2, width, per), BF16)
    return pl.pallas_call(
        down_kernel,
        out_shape=(shape, shape),
        in_specs=[SMEM] + [HBM] * 3 + [ANY],
        out_specs=[ANY, ANY],
        scratch_shapes=[
            pltpu.VMEM(g.shape, BF16),
            pltpu.VMEM(b.shape, BF16),
            pltpu.VMEM((n, rows, per), BF16),
            pltpu.VMEM((n, width, per), BF16),
            pltpu.SemaphoreType.DMA((n,)),
            pltpu.SemaphoreType.DMA((n + 2,)),
        ],
        compiler_params=params(12 << 20),
        cost_estimate=cost(COST_DOWN),
        name="down_partials",
    )(members, g, b, tokens, after)


def spread_kernel(members, b, *refs):
    gs, spread, up = refs[:INNER], refs[-2], refs[-1]
    width, depth = b.shape
    rows = gs[0].shape[0]
    planes, piece, per = up.shape
    half, cols = width // 2, depth // 2
    across = cols // per
    z, q = where_am_i()
    total = jnp.zeros((half, cols), F32)
    for j in range(INNER):
        first = (z * INNER + (q ^ j)) * (rows // BLOCK)
        wide = nt(gs[j][:, :depth], b[...])
        owner = member_of_rows(members, first, (rows, width), 0)
        column = lax.broadcasted_iota(jnp.int32, (rows, width), 1) // ADAPTER_RANK
        spread[j] = jnp.where(owner == column, adapter_scale * wide, 0.0).astype(BF16)
        hidden = gs[j][:, depth:]
        column = column[:, :half] + (q // 2) * (half // ADAPTER_RANK)
        hidden = jnp.where(owner[:, :half] == column, hidden, jnp.zeros_like(hidden))
        total = total + tn(hidden, gs[j][:, pl.ds(pl.multiple_of((q % 2) * cols, cols), cols)])
    total = (adapter_scale * total).astype(BF16)
    for t in range(planes):
        row, col = t // across * piece, t % across * per
        up[t] = total[row : row + piece, col : col + per]


def spread_rows(members, b, gs, per, planes, after):
    rows, (width, depth) = gs[0].shape[0], b.shape
    return pl.pallas_call(
        spread_kernel,
        out_shape=(
            jax.ShapeDtypeStruct((INNER, rows, width), BF16),
            jax.ShapeDtypeStruct((planes, width * depth // (INNER * planes * per), per), BF16),
        ),
        in_specs=[SMEM] + [VMEM] * (1 + INNER) + [ANY] * len(after),
        out_specs=[VMEM, VMEM],
        compiler_params=params(8 << 20),
        cost_estimate=cost(COST_SPREAD),
        name="spread_rows",
    )(members, b, *gs, *after)


def on_choice(turn, options, act):
    planes = lax.axis_size("dp") // INNER
    z, _ = where_am_i()
    for i, option in enumerate(options):
        hit = functools.reduce(
            jnp.logical_or,
            [z == p for p in range(planes) if source(turn, p, planes) == option],
        )
        pl.when(hit)(functools.partial(act, i))


def part_index(side):
    if side in (0, 1):
        return side
    parity = lax.axis_index("groups") % 2
    return parity if side == "mine" else 1 - parity


def product_kernel(plan, n_sources, *refs):
    spread, gs, refs = refs[0], refs[1 : 1 + INNER], refs[1 + INNER :]
    sources, outs, (a, sems) = refs[:n_sources], refs[-5:-2], refs[-2:]
    _, unit, width = a.shape
    rows = gs[0].shape[0]
    weights, copies = [], []
    for h, (turn, side, split, w_at, maps_at) in enumerate(plan):
        index = part_index(side) if split > 1 else 0
        if turn:
            weights.append(sources[w_at])
            depth = sources[w_at].shape[1]
            cols = pl.ds(pl.multiple_of(depth + index * width, width), width)

            def maps(i, h=h, cols=cols, maps_at=maps_at):
                return pltpu.make_async_copy(
                    sources[maps_at[i][1]].at[:, cols], a.at[h], sems.at[h]
                )

            on_choice(turn, [o for o, _ in maps_at], lambda i, maps=maps: maps(i).start())
            copies.append(maps(0))
        else:
            at = slice(index * unit, (index + 1) * unit)
            weights.append(sources[w_at].at[at])
            copies.append(pltpu.make_async_copy(sources[maps_at].at[at], a.at[h], sems.at[h]))
            copies[-1].start()
    for copy in copies:
        copy.wait()
    for j in (2, 3, 1, 0):
        for h, w in enumerate(weights):
            value = (nt(gs[j][:, : w.shape[1]], w[...]) + nt(spread[j], a[h])).astype(BF16)
            at = slice(h * unit, (h + 1) * unit)
            if j < 2:
                outs[j][:, at] = value
            else:
                outs[2][(j - 2) * rows : (j - 1) * rows, at] = value


def product(plan, sources, spread, gs, unit, after):
    rows, width = gs[0].shape[0], spread.shape[2]
    n, cols = len(plan), len(plan) * unit
    shape = jax.ShapeDtypeStruct((rows, cols), BF16)
    pair = jax.ShapeDtypeStruct((2 * rows, cols), BF16)
    weights = {w_at for _, _, _, w_at, _ in plan}
    return pl.pallas_call(
        functools.partial(product_kernel, plan, len(sources)),
        out_shape=(shape, shape, pair),
        in_specs=[VMEM] * (1 + INNER)
        + [VMEM if i in weights else ANY for i in range(len(sources))]
        + [ANY] * len(after),
        out_specs=[VMEM] * 3,
        scratch_shapes=[pltpu.VMEM((n, unit, width), BF16), pltpu.SemaphoreType.DMA((n,))],
        compiler_params=params(12 << 20),
        cost_estimate=cost(COST_MM),
        name="product",
    )(spread, *gs, *sources, *after)


def choose_kernel(turn, options, *refs):
    out, sem = refs[-2], refs[-1]
    depth = out.shape[1]

    def fetch(i):
        copy = pltpu.make_async_copy(refs[i].at[:, :depth], out, sem)
        copy.start()
        copy.wait()

    on_choice(turn, options, fetch)


def choose(turn, options, parts, depth, after, microseconds):
    half = parts[0].shape[0]
    return pl.pallas_call(
        functools.partial(choose_kernel, turn, options),
        out_shape=jax.ShapeDtypeStruct((half, depth), BF16),
        in_specs=[ANY] * (len(parts) + len(after)),
        out_specs=VMEM,
        scratch_shapes=[pltpu.SemaphoreType.DMA],
        compiler_params=params(4 << 20),
        cost_estimate=cost(microseconds),
        name="choose",
    )(*parts, *after)


def place_kernel(plan, own, core, across, both, *refs):
    out, token, sem = refs[-3:]
    rows, cols = own.shape
    unit = cols // len(plan)
    z, q = where_am_i()
    copies = []
    for h, (turn, side, split, *_) in enumerate(plan):
        index = part_index(side) if split > 1 else 0
        shard = shard_of(turn, z) * INNER
        for j, piece in enumerate((own, core, across, both)):
            at = pl.ds(pl.multiple_of(((shard + (q ^ j)) * split + index) * unit, unit), unit)
            source = piece.at[:rows, h * unit : (h + 1) * unit]
            copies.append(pltpu.make_async_copy(source, out.at[:, at], sem.at[h, j]))
            copies[-1].start()
    token[...] = jnp.zeros(token.shape, F32)
    for copy in copies:
        copy.wait()


def place(plan, pieces, out, shape, after, microseconds=COST_PLACE):
    given = [] if out is None else [out]
    return pl.pallas_call(
        functools.partial(place_kernel, plan),
        out_shape=(shape, jax.ShapeDtypeStruct((8, 128), F32)),
        in_specs=[VMEM] * INNER + [ANY] * (len(given) + len(after)),
        out_specs=[ANY, VMEM],
        scratch_shapes=[pltpu.SemaphoreType.DMA((len(plan), INNER))],
        input_output_aliases={INNER: 0} if given else {},
        compiler_params=params(6 << 20),
        cost_estimate=cost(microseconds),
        name="place",
    )(*pieces, *given, *after)


def start_loads(keep, got, up, came, t, block, sems):
    width = keep.shape[1]
    copies = [
        pltpu.make_async_copy(keep.at[2 * t + i], block.at[0, i * width : (i + 1) * width], sems.at[i])
        for i in range(2)
    ] + [
        pltpu.make_async_copy(got.at[2 * t + i], block.at[1, i * width : (i + 1) * width], sems.at[2 + i])
        for i in range(2)
    ]
    copies.append(pltpu.make_async_copy(up.at[t], block.at[0, 2 * width :], sems.at[4]))
    for i, c in enumerate(came):
        copies.append(pltpu.make_async_copy(c, block.at[2 + i], sems.at[5 + i]))
    for copy in copies:
        copy.start()
    return copies


def add_up(block, width, n_came):
    values = []
    for at in (slice(0, width), slice(width, 2 * width), slice(2 * width, None)):
        value = block[0, at].astype(F32)
        if at.stop:
            value = value + block[1, at].astype(F32)
        for i in range(n_came):
            value = value + block[2 + i, at].astype(F32)
        values.append(value)
    return values


def term_kernel(step, links, n_came, *refs):
    came, (keep, got, up), refs = refs[:n_came], refs[n_came : n_came + 3], refs[n_came + 3 :]
    n = len(links)
    width = keep.shape[1]
    outs, block, sems = refs[-2 - n : -2], refs[-2], refs[-1]
    planes = lax.axis_size("dp") // INNER
    z, _ = where_am_i()
    given, loads = list(came), []
    for i, (link, has) in enumerate(links):
        t = jnp.clip(jnp.where(z % 2 == link, z + step, z - step), 0, planes - 1)
        before = [given.pop(0)] if has else []
        loads.append(start_loads(keep, got, up, before, t, block.at[i], sems.at[i]))
    for i, (link, has) in enumerate(links):
        for copy in loads[i]:
            copy.wait()
        first, second, value = add_up(block.at[i], width, 1 if has else 0)
        outs[i][:width] = first.astype(BF16)
        outs[i][width : 2 * width] = second.astype(BF16)
        outs[i][2 * width :] = value.astype(BF16)


def terms(step, links, came, keep, got, up, after):
    rows = 2 * keep.shape[1] + up.shape[1]
    shape = jax.ShapeDtypeStruct((rows, keep.shape[2]), BF16)
    return pl.pallas_call(
        functools.partial(term_kernel, step, links, len(came)),
        out_shape=(shape,) * len(links),
        in_specs=[ANY] * (len(came) + 3 + len(after)),
        out_specs=[VMEM] * len(links),
        scratch_shapes=[
            pltpu.VMEM((len(links), 3, *shape.shape), BF16),
            pltpu.SemaphoreType.DMA((len(links), 6)),
        ],
        compiler_params=params(10 << 20),
        cost_estimate=cost(COST_TERM),
        name="running_sums",
    )(*came, keep, got, up, *after)


def total_kernel(n_came, *refs):
    came, (keep, got, up), refs = refs[:n_came], refs[n_came : n_came + 3], refs[n_came + 3 :]
    send, kept, piece, block, sems = refs[-5:]
    z, q = where_am_i()
    for copy in start_loads(keep, got, up, came, z, block, sems):
        copy.wait()
    first, second, value = add_up(block, keep.shape[1], n_came)
    low = q // 2 == 0
    kept[...] = jnp.where(low, first, second)
    send[...] = jnp.where(low, second, first).astype(BF16)
    piece[...] = value.astype(BF16)


def totals(came, keep, got, up, after):
    rows = 2 * keep.shape[1] + up.shape[1]
    return pl.pallas_call(
        functools.partial(total_kernel, len(came)),
        out_shape=(
            jax.ShapeDtypeStruct(keep.shape[1:], BF16),
            jax.ShapeDtypeStruct(keep.shape[1:], F32),
            jax.ShapeDtypeStruct(up.shape[1:], BF16),
        ),
        in_specs=[ANY] * (len(came) + 3 + len(after)),
        out_specs=[VMEM] * 3,
        scratch_shapes=[
            pltpu.VMEM((2 + len(came), rows, keep.shape[2]), BF16),
            pltpu.SemaphoreType.DMA((5 + len(came),)),
        ],
        compiler_params=params(10 << 20),
        cost_estimate=cost(COST_TERM),
        name="totals",
    )(*came, keep, got, up, *after)


def quarter_kernel(n_after, *refs):
    pieces, out = refs[: -1 - n_after], refs[-1]
    planes = len(pieces)
    rows, per = pieces[0].shape
    across = out.shape[1] // per
    z, _ = where_am_i()
    for k, piece in enumerate(pieces):
        t = (z - k + planes) % planes
        row = pl.ds(pl.multiple_of(t // across * rows, rows), rows)
        col = pl.ds(pl.multiple_of(t % across * per, per), per)
        out[row, col] = piece[...]


def quarter(pieces, shape, after):
    return pl.pallas_call(
        functools.partial(quarter_kernel, len(after)),
        out_shape=jax.ShapeDtypeStruct(shape, BF16),
        in_specs=[VMEM] * len(pieces) + [ANY] * len(after),
        out_specs=VMEM,
        compiler_params=params(2 << 20),
        cost_estimate=cost(1),
        name="quarter",
    )(*pieces, *after)


def finish_down_kernel(kept, other, *refs):
    refs[-1][...] = (kept[...] + other[...].astype(F32)).T


def finish_down(kept, other, after):
    return pl.pallas_call(
        finish_down_kernel,
        out_shape=jax.ShapeDtypeStruct(kept.shape[::-1], F32),
        in_specs=[VMEM] * 2 + [ANY] * len(after),
        out_specs=VMEM,
        compiler_params=params(4 << 20),
        cost_estimate=cost(COST_DOWN_END),
        name="finish_down",
    )(kept, other, *after)


def finish_up_kernel(q0, q1, q2, q3, after, up):
    del after
    rows, cols = q0.shape
    _, q = where_am_i()
    for j, part in enumerate((q0, q1, q2, q3)):
        row = pl.ds(pl.multiple_of((q ^ j) // 2 * rows, rows), rows)
        col = pl.ds(pl.multiple_of((q ^ j) % 2 * cols, cols), cols)
        up[row, col] = part[...].astype(F32)


def finish_up(quarters, after):
    rows, cols = quarters[0].shape
    return pl.pallas_call(
        finish_up_kernel,
        out_shape=jax.ShapeDtypeStruct((2 * rows, 2 * cols), F32),
        in_specs=[VMEM] * 4 + [ANY],
        out_specs=VMEM,
        compiler_params=params(4 << 20),
        cost_estimate=cost(1),
        name="finish_up",
    )(*quarters, *after)


def source(turn, z, planes):
    both = min(z, planes - 1 - z)
    if turn <= 2 * both:
        return (turn + 1) // 2, 1 - turn % 2
    even_is_far = (z % 2 == 0) == (z < planes // 2)
    return turn - both, 0 if even_is_far else 1


def far_plane(z, step, link):
    return z + step if z % 2 == link else z - step


def shard_of(turn, z):
    planes = lax.axis_size("dp") // INNER
    result = z
    if turn:
        for plane in range(planes):
            step, link = source(turn, plane, planes)
            result = jnp.where(z == plane, far_plane(plane, step, link), result)
    return result


def edges(step, link, planes):
    pairs = []
    for z in range(planes):
        right = z % 2 == link
        origin, to = (z - step + 1, z + 1) if right else (z + step - 1, z - 1)
        if 0 <= origin < planes and 0 <= to < planes:
            pairs.append((z, to))
    return pairs


def local(tokens, output_gradient, hidden, frozen, down_maps, up_maps, members):
    n = lax.axis_size("dp")
    groups = lax.axis_size("groups")
    planes = n // INNER
    per = frozen.shape[0]
    rows = tokens.shape[0]
    width, depth = up_maps.shape
    split = 2 if per % 256 == 0 and groups % 2 == 0 else 1
    unit = per // split

    def inner(x, bit):
        return lax.ppermute(x, "dp", [(i, i ^ bit) for i in range(n)])

    def along(x, pairs):
        return lax.ppermute(
            x, "dp", [(s * INNER + i, t * INNER + i) for s, t in pairs for i in range(INNER)]
        )

    def twin(x):
        return lax.ppermute(x, "groups", [(i, i ^ 1) for i in range(groups)])

    held = {}

    def pass_on(k):
        for link in (0, 1):
            if k > 1 and (k - 1, link) in held:
                held[k - 1, link] = hold(held[k - 1, link], mine[k - 1])
        for link in (0, 1):
            pairs = edges(k, link, planes) if k < planes else []
            if pairs:
                held[k, link] = along(held[k - 1, 1 - link], pairs)

    came = {}

    def add_on(k, keep, got, up, after):
        links = [l for l in (0, 1) if edges(k, l, planes)]
        got_before = [came[k + 1, 1 - l] for l in links if (k + 1, 1 - l) in came]
        flags = [(l, (k + 1, 1 - l) in came) for l in links]
        values = terms(k, flags, got_before, keep, got, up, after)
        for link, value in zip(links, values):
            came[k, link] = along(value, [(t, s) for s, t in edges(k, link, planes)])
        return values[0]

    at = lax.axis_index("groups") % split * unit
    maps = [down_maps[i * unit : (i + 1) * unit] for i in range(split)]
    part = jnp.concatenate([lax.dynamic_slice_in_dim(frozen, at, unit), *maps], axis=1)
    hidden = hidden_pair(hidden.T, part)
    packed = jnp.concatenate([output_gradient, hidden], axis=1)
    held[0, 0] = held[0, 1] = part
    g2 = inner(packed, 2)
    pass_on(1)
    g1 = inner(packed, 1)
    send, keep = down_partials(members, output_gradient, up_maps, tokens, per, n, g1)
    got = inner(send, 1)
    g2 = hold(g2, send)
    g3 = inner(g2, 1)
    gs = [packed, g1, g2, g3]

    out_shape = jax.ShapeDtypeStruct(tokens.shape, BF16)

    def hand_on(turn, after):
        own, core, across = pieces[turn]
        if after is not None:
            across = hold(across, after)
        pieces[turn] = own, core, across, inner(across[rows:], 1)

    mine, theirs, plans, pieces = {}, {}, {}, {}
    result, token = None, send

    def shard_options(turn):
        options = sorted({source(turn, p, planes) for p in range(planes)})
        return options, [held[o] for o in options]

    def multiply(k, spread, after):
        sources, plan = [], []

        def add(x):
            sources.append(x)
            return len(sources) - 1

        def add_part(turn, side, w):
            options, parts = shard_options(turn)
            maps = [(option, add(x)) for option, x in zip(options, parts)]
            plan.append((turn, side, split, add(w), maps))

        if k == 1:
            at = add(frozen), add(down_maps)
            plan += [(0, i, split, *at) for i in range(split)]
        elif split > 1:
            add_part(k - 1, "theirs", theirs[k - 1])
        if k < planes:
            add_part(k, "mine", mine[k])
        if not plan:
            return after[0]
        plans[k] = plan
        blocks = product(plan, sources, spread, gs, unit, after)
        pieces[k] = blocks[0], inner(blocks[1], 1), inner(blocks[2], 2)
        return blocks[0]

    def hand_on(k, *after, microseconds=0):
        own, core, across = pieces[k]
        across = hold(across, *after, microseconds=microseconds)
        pieces[k] = own, core, across, inner(across[rows:], 1)
        return across

    last = send
    for k in range(1, planes):
        options, parts = shard_options(k)
        waits = [held[k, l] for l in (0, 1) if (k, l) in held]
        waits += [theirs[k - 1]] if k - 1 in theirs else []
        waits += [came[planes - k + 1, l] for l in (0, 1) if (planes - k + 1, l) in came]
        price = COST_CHOOSE if k == 1 else 1
        mine[k] = choose(k, options, parts, depth, waits + [last, token], price)
        pass_on(k + 1)
        if split > 1:
            theirs[k] = twin(mine[k])
        if k == 1:
            spread, up = spread_rows(members, up_maps, gs, per, planes, [mine[1]])
        summed = add_on(planes - k, keep, got, up, [mine[k]])
        across = hand_on(k - 1, summed) if k > 1 else summed
        last = multiply(k, spread, [across])
        if k > 1:
            result, token = place(plans[k - 1], pieces[k - 1], result, out_shape, [last])
    if planes - 1 in theirs:
        theirs[planes - 1] = last = hold(theirs[planes - 1], last, microseconds=COST_TWIN)
    if planes > 1:
        last = hand_on(planes - 1, last, token)
    came_last = [came[1, l] for l in (0, 1) if (1, l) in came]
    last = multiply(planes, spread, [last])
    down_send, down_kept, piece = totals(came_last, keep, got, up, [last])
    other = inner(down_send, 2)
    moved = [
        along(piece, [(s, (s + k) % planes) for s in range(planes)]) for k in range(1, planes)
    ]
    if planes > 1:
        result, token = place(plans[planes - 1], pieces[planes - 1], result, out_shape, [last])
    mine_up = quarter([piece, *moved], (width // 2, depth // 2), [token])
    over_y = inner(mine_up, 2)
    down_grad = finish_down(down_kept, other, [mine_up])
    quarters = [mine_up, inner(mine_up, 1), over_y, inner(over_y, 1)]
    if planes in plans:
        hand_on(planes, microseconds=COST_HAND)
        result, token = place(plans[planes], pieces[planes], result, out_shape, [], COST_LAST)
    up_grad = finish_up(quarters, [token])
    return result, down_grad, up_grad


def solution(mesh):
    in_specs = (
        P(("groups", "dp"), None),
        P(("groups", "dp"), None),
        P(("groups", "dp"), None),
        P("dp", None),
        P(("groups", "dp"), None),
        P("groups", None),
        P("groups"),
    )
    out_specs = (P(("groups", "dp"), None), P(("groups", "dp"), None), P("groups", None))
    return jax.shard_map(local, mesh=mesh, in_specs=in_specs, out_specs=out_specs, check_vma=False)
```
